768 devices in a mesh: section: 32 (over y_hi, x, core), peer: 24 (over z, y_lo).
Axes of the slice: x: 4, y: 8 (y_hi: 4, y_lo: 2; y = y_hi * 2 + y_lo), z: 12, core: 2. Of those that a mesh axis runs over, the one named last changes fastest.
Arguments:
- stash: bfloat16 [32, 24, 18, 8, 5120], P('section', 'peer'), may hold values from -134 to 134
- back_in: bfloat16 [32, 24, 18, 8, 5120], P('section', 'peer'), may hold values from -6 to 6
- down_proj: bfloat16 [32, 144, 5120], P('section'), may hold values from -0.078125 to 0.078125
- up_proj: bfloat16 [32, 144, 5120], P('section'), may hold values from -0.5 to 0.5
- gain: float32 [32, 5120], P('section'), may hold values from 0.5 to 1.5
- sent_to: int32 [32, 24, 18], P('section', 'peer'), may hold values from 0 to 23, as said below
- sent_count: int32 [32, 24], P('section', 'peer'), may hold values from 14 to 18, as said below
- recv_from: int32 [32, 24, 18], P('section', 'peer'), may hold values from 0 to 23, as said below
- back_live: int32 [32, 24, 18], P('section', 'peer'), may hold values from 0 to 1, as said below
Outputs:
- returned: bfloat16 [32, 24, 18, 8, 5120], P('section', 'peer')
- grad_down: bfloat16 [32, 144, 5120], P('section')
- grad_up: bfloat16 [32, 144, 5120], P('section')
The draws below stay inside these ranges and needn't reach their ends.
Inputs may be any that keep to these rules, and one draw needn't show every extreme that they name: `sent_to`: the 18 slots of one device name distinct peers. `sent_count`: uneven over peers; on every section some peer has 18. `recv_from`: the 18 slots of one device name distinct peers. Peer c of section s - 1 (the last section before section 0) names peer a of section s in one of its first sent_count slots exactly when some slot of recv_from at (s, a) names c with back_live 1. `back_live`: on every section some device has all 18 slots live.
All inputs are finite; a program needn't handle non-finite values.
Results may differ from the reference program's by a relative error of at most 0.028.
Values may be sent and summed in bfloat16 or wider, within the bound.
No kernel may reach another device: no remote copies, remote signals or barrier semaphores. Data moves between devices by JAX's collectives and lax.ppermute only.
A program may use at most 64 MiB of HBM per device.

```python
import math
import jax
import jax.numpy as jnp
from jax import lax

D = 5120
RANK = 144
MB = 8
SEND = 18
N_SECTION = 32
N_PEER = 24


def wiring(key):
    key_off = jax.random.fold_in(key, 101)
    key_order = jax.random.fold_in(key, 102)
    key_count = jax.random.fold_in(key, 103)
    key_full = jax.random.fold_in(key, 104)
    key_recv = jax.random.fold_in(key, 105)
    peer_index = jnp.arange(N_PEER, dtype=jnp.int32)
    slot_index = jnp.arange(SEND, dtype=jnp.int32)
    off_scores = jax.random.randint(key_off, (N_SECTION, N_PEER), 0, 2 ** 20) * N_PEER + peer_index[None, :]
    unused, offsets = lax.top_k(off_scores, SEND)
    offsets = offsets.astype(jnp.int32)
    order_scores = jax.random.randint(key_order, (N_SECTION, N_PEER, SEND), 0, 2 ** 20) * SEND + slot_index[None, None, :]
    unused, order = lax.top_k(order_scores, SEND)
    order = order.astype(jnp.int32)
    full_recv = jax.random.randint(key_recv, (N_SECTION,), 0, N_PEER).astype(jnp.int32)
    needed = (full_recv[:, None] - peer_index[None, :]) % N_PEER
    match = offsets[:, None, :] == needed[:, :, None]
    found = jnp.any(match, axis=2)
    wanted = jnp.sum(match.astype(jnp.int32) * slot_index[None, None, :], axis=2).astype(jnp.int32)
    first = order[:, :, 0]
    swapped = jnp.where(order == wanted[:, :, None], first[:, :, None], jnp.where(slot_index[None, None, :] == 0, wanted[:, :, None], order))
    order = jnp.where(found[:, :, None], swapped, order).astype(jnp.int32)
    lowest = max(1, SEND - max(1, SEND // 4))
    live_count = jax.random.randint(key_count, (N_SECTION, N_PEER), lowest, SEND + 1)
    full_peer = jax.random.randint(key_full, (N_SECTION,), 0, N_PEER)
    live_count = jnp.where(peer_index[None, :] == full_peer[:, None], SEND, live_count).astype(jnp.int32)
    offsets_wide = jnp.broadcast_to(offsets[:, None, :], (N_SECTION, N_PEER, SEND))
    picked = jnp.take_along_axis(offsets_wide, order, axis=2)
    routes = ((peer_index[None, :, None] + picked) % N_PEER).astype(jnp.int32)
    position = jnp.sum((order[:, :, :, None] == slot_index[None, None, None, :]).astype(jnp.int32) * slot_index[None, None, :, None], axis=2)
    live_send = (position < live_count[:, :, None]).astype(jnp.int32)
    senders = ((peer_index[None, :, None] - offsets[:, None, :]) % N_PEER).astype(jnp.int32)
    live_recv = jnp.take_along_axis(live_send, senders, axis=1)
    recv_from = jnp.roll(senders, 1, axis=0).astype(jnp.int32)
    back_live = jnp.roll(live_recv, 1, axis=0).astype(jnp.int32)
    return (routes, live_count, recv_from, back_live)


def draw_sent_to(key, part):
    routes, live_count, recv_from, back_live = wiring(key)
    return routes


def draw_sent_count(key, part):
    routes, live_count, recv_from, back_live = wiring(key)
    return live_count


def draw_recv_from(key, part):
    routes, live_count, recv_from, back_live = wiring(key)
    return recv_from


def draw_back_live(key, part):
    routes, live_count, recv_from, back_live = wiring(key)
    return back_live


def draw_stash(key, part):
    key = jax.random.fold_in(key, 11)
    key_base = jax.random.fold_in(key, 1)
    key_column = jax.random.fold_in(key, 2)
    key_row = jax.random.fold_in(key, 3)
    shape = (N_SECTION, N_PEER, SEND, MB, D)
    column = jnp.exp(jax.random.uniform(key_column, (N_SECTION, 1, 1, 1, D), dtype=jnp.float32) * math.log(10.0))
    rowscale = jnp.exp(jax.random.uniform(key_row, (N_SECTION, N_PEER, SEND, MB, 1), dtype=jnp.float32) * math.log(10.0))
    base = jax.random.truncated_normal(key_base, -4.0, 4.0, shape, dtype=jnp.float32)
    return (base * column * rowscale / 3.0).astype(jnp.bfloat16)


def block_levels(rng, dims, pieces, low, largest):
    level, own = 1.0, jax.random.fold_in(rng, 6)
    for dim, blocks in pieces:
        draws = jnp.exp(jax.random.uniform(jax.random.fold_in(own, dim), (blocks,), jnp.float32, low / len(pieces), largest / len(pieces)))
        level = level * jnp.repeat(draws, dims[dim] // blocks).reshape([-1 if axis == dim else 1 for axis in range(len(dims))])
    return level


def scatter_about(rng, dims, width, bound, cuts=(), held_as=jnp.bfloat16):
    drawn = jax.random.normal(rng, dims, jnp.float32) * width
    if len(cuts) > 0:
        drawn = block_levels(rng, dims, cuts, -0.22, 0.18) * drawn
    return jnp.clip(drawn, min=-bound, max=bound).astype(held_as)


def setup_inputs(seed: int = 0) -> dict:
    arg_keys = jax.random.split(jax.random.key(seed), 10)
    return {
        "stash": draw_stash(jax.random.fold_in(arg_keys[9], 71), 0),
        "back_in": scatter_about(arg_keys[1], (N_SECTION, N_PEER, SEND, MB, D), 1.0, 6.0, ((0, 32), (1, 24))),
        "down_proj": scatter_about(arg_keys[2], (N_SECTION, RANK, D), D ** -0.5, 0.078125, ((0, 32),)),
        "up_proj": scatter_about(arg_keys[3], (N_SECTION, RANK, D), RANK ** -0.5, 0.5, ((0, 32),)),
        "gain": jnp.clip(1.0 + 0.1 * jax.random.normal(arg_keys[4], (N_SECTION, D), jnp.float32), 0.5, 1.5),
        "sent_to": draw_sent_to(jax.random.fold_in(arg_keys[9], 71), 0),
        "sent_count": draw_sent_count(jax.random.fold_in(arg_keys[9], 71), 0),
        "recv_from": draw_recv_from(jax.random.fold_in(arg_keys[9], 71), 0),
        "back_live": draw_back_live(jax.random.fold_in(arg_keys[9], 71), 0),
    }


epsilon = 1e-05

def section_backward(items):
    stash, back_in, back_live, recv_from, down_proj, up_proj, gain, prev_sent, prev_count = items
    slot_mask = back_live.astype(jnp.bfloat16)[:, :, None, None]
    stored = stash * slot_mask
    incoming = back_in * slot_mask
    peer_count, slot_count, micro_rows, model_width = stored.shape
    stored = stored.reshape(peer_count, slot_count * micro_rows, model_width)
    incoming = incoming.reshape(peer_count, slot_count * micro_rows, model_width)
    stored_f = stored.astype(jnp.float32)
    inverse = lax.rsqrt(lax.optimization_barrier(jnp.mean(stored_f * stored_f, axis=-1, keepdims=True)) + epsilon)
    unit_rows = stored_f * inverse
    normed = (unit_rows * gain).astype(jnp.bfloat16)
    down_f = down_proj.astype(jnp.float32)
    up_f = up_proj.astype(jnp.float32)
    preact = jnp.einsum('prd,kd->prk', normed.astype(jnp.float32), down_f)
    sigmoid_pre = jax.nn.sigmoid(preact)
    activation = (preact * sigmoid_pre).astype(jnp.bfloat16)
    incoming_f = incoming.astype(jnp.float32)
    back_act = jnp.einsum('prd,kd->prk', incoming_f, up_f)
    back_pre = (back_act * (sigmoid_pre * (1.0 + preact * (1.0 - sigmoid_pre)))).astype(jnp.bfloat16)
    back_norm = jnp.einsum('prk,kd->prd', back_pre.astype(jnp.float32), down_f) * gain
    input_grad = incoming_f + inverse * (back_norm - unit_rows * lax.optimization_barrier(jnp.mean(back_norm * unit_rows, axis=-1, keepdims=True)))
    input_grad = input_grad.astype(jnp.bfloat16)
    part_down = jnp.einsum('prk,prd->pkd', back_pre.astype(jnp.float32), normed.astype(jnp.float32)).astype(jnp.bfloat16)
    part_up = jnp.einsum('prk,prd->pkd', activation.astype(jnp.float32), incoming_f).astype(jnp.bfloat16)
    grad_down = (lax.optimization_barrier(jnp.sum(part_down.astype(jnp.float32), axis=0)) / peer_count).astype(jnp.bfloat16)
    grad_up = (lax.optimization_barrier(jnp.sum(part_up.astype(jnp.float32), axis=0)) / peer_count).astype(jnp.bfloat16)
    input_grad = input_grad.reshape(peer_count, slot_count, micro_rows, model_width)
    peer_index = jnp.arange(peer_count, dtype=jnp.int32)
    onehot = ((recv_from.astype(jnp.int32)[:, :, None] == peer_index[None, None, :]) & (back_live[:, :, None] == 1)).astype(jnp.float32)
    by_sender = jnp.einsum('arc,armd->acmd', onehot, input_grad.astype(jnp.float32)).astype(jnp.bfloat16)
    swapped = jnp.swapaxes(by_sender, 0, 1)
    picked = jnp.take_along_axis(swapped, prev_sent.astype(jnp.int32)[:, :, None, None], axis=1)
    send_slots = prev_sent.shape[1]
    live_mask = (jnp.arange(send_slots, dtype=jnp.int32)[None, :] < prev_count[:, None]).astype(jnp.bfloat16)
    return (picked * live_mask[:, :, None, None], grad_down, grad_up)

def reference(stash, back_in, down_proj, up_proj, gain, sent_to, sent_count, recv_from, back_live):
    prev_sent = jnp.roll(sent_to, 1, axis=0)
    prev_count = jnp.roll(sent_count, 1, axis=0)
    shifted, grad_down, grad_up = lax.map(section_backward, (stash, back_in, back_live, recv_from, down_proj, up_proj, gain, prev_sent, prev_count))
    returned = jnp.roll(shifted, -1, axis=0)
    return (returned, grad_down, grad_up)
```

```python
import jax
import jax.numpy as jnp
from jax import lax
from jax.sharding import Mesh, PartitionSpec as P

epsilon = 1e-05
SECTION = ("section",)


def permuted(block, axes, route):
    return lax.ppermute(block, axes, route)


def compact(blocks, targets, live_count):
    peer_count = blocks.shape[0]
    send_slots = targets.shape[0]
    peer_index = jnp.arange(peer_count, dtype=jnp.int32)
    slot_index = jnp.arange(send_slots, dtype=jnp.int32)
    selector = (
        (targets[:, None] == peer_index[None, :]) & (slot_index[:, None] < live_count)
    ).astype(jnp.bfloat16)
    flat = blocks.reshape(peer_count, -1)
    packed = jnp.dot(selector, flat, preferred_element_type=jnp.float32).astype(jnp.bfloat16)
    return packed.reshape((send_slots,) + blocks.shape[1:])


def on_device(stash, back_in, down_proj, up_proj, gain, sent_to, sent_count, recv_from, back_live):
    peer_count = 24
    live_slots = back_live[0, 0]
    slot_mask = live_slots.astype(jnp.bfloat16)[:, None, None]
    slot_count = stash.shape[2]
    micro_rows = stash.shape[3]
    model_width = stash.shape[4]
    rank = down_proj.shape[1]
    stored = (stash[0, 0] * slot_mask).reshape(slot_count * micro_rows, model_width)
    incoming = (back_in[0, 0] * slot_mask).reshape(slot_count * micro_rows, model_width)
    section_gain = gain[0]
    down_local = down_proj[0]
    up_local = up_proj[0]
    stored_f = stored.astype(jnp.float32)
    inverse = lax.rsqrt(jnp.mean(stored_f * stored_f, axis=-1, keepdims=True) + epsilon)
    unit_rows = stored_f * inverse
    normed = (unit_rows * section_gain).astype(jnp.bfloat16)
    contract_last = (((1,), (1,)), ((), ()))
    contract_rows = (((0,), (0,)), ((), ()))
    preact = lax.dot_general(normed, down_local, contract_last, preferred_element_type=jnp.float32)
    sigmoid_pre = jax.nn.sigmoid(preact)
    activation = (preact * sigmoid_pre).astype(jnp.bfloat16)
    back_act = lax.dot_general(
        incoming, up_local, contract_last, preferred_element_type=jnp.float32
    )
    back_pre = (back_act * (sigmoid_pre * (1.0 + preact * (1.0 - sigmoid_pre)))).astype(
        jnp.bfloat16
    )
    part_down = lax.dot_general(
        back_pre, normed, contract_rows, preferred_element_type=jnp.float32
    ).astype(jnp.bfloat16)
    part_up = lax.dot_general(
        activation, incoming, contract_rows, preferred_element_type=jnp.float32
    ).astype(jnp.bfloat16)
    parts = jnp.concatenate([part_down, part_up], axis=0)
    piece = lax.psum_scatter(parts, "z", scatter_dimension=0, tiled=True)

    back_norm = jnp.dot(back_pre, down_local, preferred_element_type=jnp.float32) * section_gain
    input_grad = incoming.astype(jnp.float32) + inverse * (
        back_norm - unit_rows * jnp.mean(back_norm * unit_rows, axis=-1, keepdims=True)
    )
    input_grad = input_grad.astype(jnp.bfloat16)
    peer_index = jnp.arange(peer_count, dtype=jnp.int32)
    spreader = (
        (recv_from[0, 0][None, :] == peer_index[:, None]) & (live_slots[None, :] == 1)
    ).astype(jnp.bfloat16)
    by_sender = jnp.dot(
        spreader, input_grad.reshape(slot_count, -1), preferred_element_type=jnp.float32
    ).astype(jnp.bfloat16)
    by_sender = by_sender.reshape(peer_count, micro_rows, model_width)
    exchanged = lax.all_to_all(by_sender, ("z", "yl"), split_axis=0, concat_axis=0, tiled=True)
    back = [((i + 1) % 32, i) for i in range(32)]
    arrived = lax.ppermute(exchanged, "section", back)
    returned = compact(arrived, sent_to[0, 0], sent_count[0, 0])

    half = model_width // 2
    quarter = half // 2
    y = lax.axis_index("yl")
    other = [(0, 1), (1, 0)]
    keep = lax.dynamic_slice_in_dim(piece, y * half, half, 1)
    give = lax.dynamic_slice_in_dim(piece, (1 - y) * half, half, 1)
    got = lax.ppermute(give, "yl", other)
    total = ((keep.astype(jnp.float32) + got.astype(jnp.float32)) / peer_count).astype(jnp.bfloat16)
    mine, theirs = [], []
    for c in range(2):
        whole = lax.all_gather(total[:, c * quarter : (c + 1) * quarter], "z", axis=0, tiled=True)
        mine.append(whole)
        theirs.append(lax.ppermute(whole, "yl", other))
    low = [jnp.where(y == 0, a, b) for a, b in zip(mine, theirs)]
    high = [jnp.where(y == 0, b, a) for a, b in zip(mine, theirs)]
    grads = jnp.concatenate(low + high, axis=1)
    return (returned[None, None], grads[None, :rank], grads[None, rank:])


def solution(mesh):
    inner = Mesh(mesh.devices.reshape(32, 12, 2), ("section", "z", "yl"))
    peer = ("z", "yl")
    placed = (
        P("section", peer, None, None, None),
        P("section", peer, None, None, None),
        P("section", None, None),
        P("section", None, None),
        P("section", None),
        P("section", peer, None),
        P("section", peer),
        P("section", peer, None),
        P("section", peer, None),
    )
    return jax.shard_map(
        on_device,
        mesh=inner,
        in_specs=placed,
        out_specs=(
            P("section", peer, None, None, None),
            P("section", None, None),
            P("section", None, None),
        ),
        check_vma=False,
    )
```

```python
import jax
import jax.numpy as jnp
from jax import lax
from jax.experimental import pallas as pl
from jax.experimental.pallas import tpu as pltpu
from jax.sharding import Mesh, PartitionSpec as P

epsilon = 1e-05
SECTIONS, Z, Y = 32, 12, 2
PEERS = Z * Y
SLOTS, MB, D, RANK = 18, 8, 5120, 144
ROWS = SLOTS * MB
HALF = D // 2
CHUNK = 512
WIDE = 1792
NARROW = HALF - WIDE
LAST = (((1,), (1,)), ((), ()))
FIRST = (((0,), (0,)), ((), ()))
VMEM_LIMIT = 60 * 2**20


def _chunks(width, step):
    return [slice(c, c + step) for c in range(0, width, step)]


def _local(
    y_ref, recv_ref, live_ref, gain, stash_hbm, back_in_hbm, down_hbm, up_hbm,
    out_hbm, give_hbm, keep_hbm,
    stash, back_in, down, up, mask, normed, out, give, keep, sems,
):
    f32, bf16 = jnp.float32, jnp.bfloat16
    pairs = ((stash_hbm, stash), (down_hbm, down), (back_in_hbm, back_in), (up_hbm, up))
    loads = [pltpu.make_async_copy(a, b, sems.at[i]) for i, (a, b) in enumerate(pairs)]
    for load in loads:
        load.start()
    for slot in range(SLOTS):
        mask[MB * slot : MB * (slot + 1), :] = jnp.full((MB, 128), live_ref[slot].astype(f32), f32)
    for peer in range(PEERS):
        out[peer] = jnp.zeros((MB, D), bf16)
    loads[0].wait()
    squares = jnp.zeros((ROWS, 128), f32)
    for cols in _chunks(D, 128):
        s = stash[:, cols].astype(f32)
        squares += s * s
    live = mask[:, :1]
    inverse = lax.rsqrt(jnp.sum(squares, axis=1, keepdims=True) * (1.0 / D) + epsilon) * live
    for load in loads[1:]:
        load.wait()
    preact = jnp.zeros((ROWS, RANK), f32)
    back_act = jnp.zeros((ROWS, RANK), f32)
    for cols in _chunks(D, CHUNK):
        n = (stash[:, cols].astype(f32) * inverse * gain[:, cols]).astype(bf16)
        normed[:, cols] = n
        preact += lax.dot_general(n, down[:, cols], LAST, preferred_element_type=f32)
        back_act += lax.dot_general(back_in[:, cols], up[:, cols], LAST, preferred_element_type=f32)
    sigmoid = 1.0 / (1.0 + jnp.exp(-preact))
    act = (preact * sigmoid).astype(bf16)
    pre = (back_act * live * (sigmoid * (1.0 + preact * (1.0 - sigmoid)))).astype(bf16)
    shared = jnp.sum(pre.astype(f32) * preact, axis=1, keepdims=True) * (inverse * (1.0 / D))
    alive = live > 0.5
    for cols in _chunks(D, CHUNK):
        back_norm = jnp.dot(pre, down[:, cols], preferred_element_type=f32) * gain[:, cols]
        unit = stash[:, cols].astype(f32) * inverse
        grad = back_in[:, cols].astype(f32) + inverse * back_norm - unit * shared
        grad = jnp.where(alive, grad, 0.0)
        for slot in range(SLOTS):
            out[recv_ref[slot], :, cols] = grad[MB * slot : MB * (slot + 1), :].astype(bf16)
    stores = [pltpu.make_async_copy(out, out_hbm, sems.at[4])]
    stores[0].start()
    y = y_ref[0]
    for place, target, half in ((give, give_hbm, 1 - y), (keep, keep_hbm, y)):
        for cols in _chunks(HALF, CHUNK):
            here = pl.ds(pl.multiple_of(half * HALF + cols.start, 128), CHUNK)
            place[:RANK, cols] = lax.dot_general(
                pre, normed[:, here], FIRST, preferred_element_type=f32
            ).astype(bf16)
            place[RANK:, cols] = lax.dot_general(
                act, back_in[:, here], FIRST, preferred_element_type=f32
            ).astype(bf16)
        stores.append(pltpu.make_async_copy(place, target, sems.at[4 + len(stores)]))
        stores[-1].start()
    for store in stores:
        store.wait()


def local(y, recv, live, gain, stash, back_in, down, up):
    smem = pl.BlockSpec(memory_space=pltpu.SMEM)
    vmem = pl.BlockSpec(memory_space=pltpu.VMEM)
    hbm = pl.BlockSpec(memory_space=pl.ANY)
    bf16 = jnp.bfloat16
    outs = ((PEERS, MB, D), (2 * RANK, HALF), (2 * RANK, HALF))
    return pl.pallas_call(
        _local,
        out_shape=tuple(jax.ShapeDtypeStruct(shape, bf16) for shape in outs),
        in_specs=[smem, smem, smem, vmem] + [hbm] * 4,
        out_specs=[hbm] * 3,
        scratch_shapes=[
            pltpu.VMEM((ROWS, D), bf16),
            pltpu.VMEM((ROWS, D), bf16),
            pltpu.VMEM((RANK, D), bf16),
            pltpu.VMEM((RANK, D), bf16),
            pltpu.VMEM((ROWS, 128), jnp.float32),
            pltpu.VMEM((ROWS, D), bf16),
        ]
        + [pltpu.VMEM(shape, bf16) for shape in outs]
        + [pltpu.SemaphoreType.DMA((7,))],
        compiler_params=pltpu.CompilerParams(vmem_limit_bytes=VMEM_LIMIT),
        cost_estimate=pl.CostEstimate(
            flops=10 * ROWS * RANK * D, bytes_accessed=16 * ROWS * D, transcendentals=ROWS * RANK
        ),
        name="local",
    )(y, recv, live, gain, stash, back_in, down, up)


def _compact(wiring, blocks, out, sems):
    for slot in range(SLOTS):

        @pl.when(slot < wiring[SLOTS])
        def _(slot=slot):
            pltpu.make_async_copy(blocks.at[wiring[slot]], out.at[slot], sems.at[slot]).start()

    for slot in range(SLOTS):
        live = slot < wiring[SLOTS]

        @pl.when(jnp.logical_not(live))
        def _(slot=slot):
            out[slot] = jnp.zeros((MB, D), jnp.bfloat16)

        @pl.when(live)
        def _(slot=slot):
            pltpu.make_async_copy(blocks.at[wiring[slot]], out.at[slot], sems.at[slot]).wait()


def compact(wiring, blocks):
    return pl.pallas_call(
        _compact,
        out_shape=jax.ShapeDtypeStruct((SLOTS, MB, D), jnp.bfloat16),
        in_specs=[pl.BlockSpec(memory_space=pltpu.SMEM), pl.BlockSpec(memory_space=pl.ANY)],
        out_specs=pl.BlockSpec(memory_space=pltpu.VMEM),
        scratch_shapes=[pltpu.SemaphoreType.DMA((SLOTS,))],
        compiler_params=pltpu.CompilerParams(vmem_limit_bytes=VMEM_LIMIT),
        cost_estimate=pl.CostEstimate(flops=0, bytes_accessed=5 * ROWS * D, transcendentals=0),
        name="compact",
    )(wiring, blocks)


def on_device(stash, back_in, down_proj, up_proj, gain, sent_to, sent_count, recv_from, back_live):
    f32, bf16 = jnp.float32, jnp.bfloat16
    y = lax.axis_index("yl")
    swap = [(0, 1), (1, 0)]
    back = [((i + 1) % SECTIONS, i) for i in range(SECTIONS)]
    ahead = [(i, (i + 1) % SECTIONS) for i in range(SECTIONS)]
    stash = stash.reshape(ROWS, D)
    back_in = back_in.reshape(ROWS, D)
    live, recv = back_live[0, 0], recv_from[0, 0]
    by_sender, give, keep = local(
        y.astype(jnp.int32).reshape(1), recv, live, gain, stash, back_in, down_proj[0], up_proj[0]
    )
    exchanged = lax.all_to_all(by_sender, ("z", "yl"), split_axis=0, concat_axis=0, tiled=True)
    got = lax.ppermute(give, "yl", swap)
    wiring = lax.ppermute(jnp.concatenate([sent_to[0, 0], sent_count[0]]), "section", ahead)
    keep, wiring = lax.optimization_barrier((keep, wiring))
    pair = (keep.astype(f32) + got.astype(f32)).astype(bf16)
    shard = lax.psum_scatter(pair.reshape(180, 4096), "z", scatter_dimension=0, tiled=True)
    mean = (shard.astype(f32) / PEERS).astype(bf16).reshape(24, HALF)
    wide, narrow = mean[:, :WIDE], mean[:, WIDE:]
    narrow_got = lax.ppermute(narrow, "yl", swap)
    narrow_both = jnp.concatenate(
        [jnp.where(y == 0, narrow, narrow_got), jnp.where(y == 0, narrow_got, narrow)], axis=1
    )
    wide, exchanged = lax.optimization_barrier((wide, exchanged))
    packed = compact(wiring, exchanged)
    returned = lax.ppermute(packed, "section", back)
    wide_mine = lax.all_gather(wide, "z", axis=0, tiled=True)
    wide_got = lax.ppermute(wide_mine, "yl", swap)
    narrow_both, wide_mine, returned = lax.optimization_barrier((narrow_both, wide_mine, returned))
    narrow_all = lax.all_gather(narrow_both, "z", axis=0, tiled=True)
    grads = jnp.concatenate(
        [
            jnp.where(y == 0, wide_mine, wide_got),
            narrow_all[:, :NARROW],
            jnp.where(y == 0, wide_got, wide_mine),
            narrow_all[:, NARROW:],
        ],
        axis=1,
    )
    return (
        returned.reshape(1, 1, SLOTS, MB, D),
        grads[None, :RANK],
        grads[None, RANK:],
    )


def solution(mesh):
    inner = Mesh(mesh.devices.reshape(SECTIONS, Z, Y), ("section", "z", "yl"))
    peer = ("z", "yl")
    placed = (
        P("section", peer, None, None, None),
        P("section", peer, None, None, None),
        P("section", None, None),
        P("section", None, None),
        P("section", None),
        P("section", peer, None),
        P("section", peer),
        P("section", peer, None),
        P("section", peer, None),
    )
    return jax.shard_map(
        on_device,
        mesh=inner,
        in_specs=placed,
        out_specs=(
            P("section", peer, None, None, None),
            P("section", None, None),
            P("section", None, None),
        ),
        check_vma=False,
    )
```

```python
import jax
import jax.numpy as jnp
from jax import lax
from jax.experimental import pallas as pl
from jax.experimental.pallas import tpu as pltpu
from jax.sharding import Mesh, PartitionSpec as P

epsilon = 1e-05
SECTIONS, Z, Y = 32, 12, 2
PEERS = Z * Y
SLOTS, MB, D, RANK = 18, 8, 5120, 144
ROWS = SLOTS * MB
HALF = D // 2
CHUNK = 512
WIDE = 1792
NARROW = HALF - WIDE
LAST = (((1,), (1,)), ((), ()))
FIRST = (((0,), (0,)), ((), ()))
VMEM_LIMIT = 60 * 2**20


def _chunks(width, step):
    return [slice(c, c + step) for c in range(0, width, step)]


def _local(
    y_ref, recv_ref, live_ref, gain, stash_hbm, back_in_hbm, down_hbm, up_hbm,
    out_hbm, give_hbm, keep_hbm,
    stash, back_in, down, up, mask, normed, out, give, keep, sems,
):
    f32, bf16 = jnp.float32, jnp.bfloat16
    pairs = ((stash_hbm, stash), (down_hbm, down), (back_in_hbm, back_in), (up_hbm, up))
    loads = [pltpu.make_async_copy(a, b, sems.at[i]) for i, (a, b) in enumerate(pairs)]
    for load in loads:
        load.start()
    for slot in range(SLOTS):
        mask[MB * slot : MB * (slot + 1), :] = jnp.full((MB, 128), live_ref[slot].astype(f32), f32)
    for peer in range(PEERS):
        out[peer] = jnp.zeros((MB, D), bf16)
    loads[0].wait()
    squares = jnp.zeros((ROWS, 128), f32)
    for cols in _chunks(D, 128):
        s = stash[:, cols].astype(f32)
        squares += s * s
    live = mask[:, :1]
    inverse = lax.rsqrt(jnp.sum(squares, axis=1, keepdims=True) * (1.0 / D) + epsilon) * live
    for load in loads[1:]:
        load.wait()
    preact = jnp.zeros((ROWS, RANK), f32)
    back_act = jnp.zeros((ROWS, RANK), f32)
    for cols in _chunks(D, CHUNK):
        n = (stash[:, cols].astype(f32) * inverse * gain[:, cols]).astype(bf16)
        normed[:, cols] = n
        preact += lax.dot_general(n, down[:, cols], LAST, preferred_element_type=f32)
        back_act += lax.dot_general(back_in[:, cols], up[:, cols], LAST, preferred_element_type=f32)
    sigmoid = 1.0 / (1.0 + jnp.exp(-preact))
    act = (preact * sigmoid).astype(bf16)
    pre = (back_act * live * (sigmoid * (1.0 + preact * (1.0 - sigmoid)))).astype(bf16)
    shared = jnp.sum(pre.astype(f32) * preact, axis=1, keepdims=True) * (inverse * (1.0 / D))
    alive = live > 0.5
    for cols in _chunks(D, CHUNK):
        back_norm = jnp.dot(pre, down[:, cols], preferred_element_type=f32) * gain[:, cols]
        unit = stash[:, cols].astype(f32) * inverse
        grad = back_in[:, cols].astype(f32) + inverse * back_norm - unit * shared
        grad = jnp.where(alive, grad, 0.0)
        for slot in range(SLOTS):
            out[recv_ref[slot], :, cols] = grad[MB * slot : MB * (slot + 1), :].astype(bf16)
    stores = [pltpu.make_async_copy(out, out_hbm, sems.at[4])]
    stores[0].start()
    y = y_ref[0]
    for place, target, half in ((give, give_hbm, 1 - y), (keep, keep_hbm, y)):
        for cols in _chunks(HALF, CHUNK):
            here = pl.ds(pl.multiple_of(half * HALF + cols.start, 128), CHUNK)
            place[:RANK, cols] = lax.dot_general(
                pre, normed[:, here], FIRST, preferred_element_type=f32
            ).astype(bf16)
            place[RANK:, cols] = lax.dot_general(
                act, back_in[:, here], FIRST, preferred_element_type=f32
            ).astype(bf16)
        stores.append(pltpu.make_async_copy(place, target, sems.at[4 + len(stores)]))
        stores[-1].start()
    for store in stores:
        store.wait()


def local(y, recv, live, gain, stash, back_in, down, up):
    smem = pl.BlockSpec(memory_space=pltpu.SMEM)
    vmem = pl.BlockSpec(memory_space=pltpu.VMEM)
    hbm = pl.BlockSpec(memory_space=pl.ANY)
    bf16 = jnp.bfloat16
    outs = ((PEERS, MB, D), (2 * RANK, HALF), (2 * RANK, HALF))
    return pl.pallas_call(
        _local,
        out_shape=tuple(jax.ShapeDtypeStruct(shape, bf16) for shape in outs),
        in_specs=[smem, smem, smem, vmem] + [hbm] * 4,
        out_specs=[hbm] * 3,
        scratch_shapes=[
            pltpu.VMEM((ROWS, D), bf16),
            pltpu.VMEM((ROWS, D), bf16),
            pltpu.VMEM((RANK, D), bf16),
            pltpu.VMEM((RANK, D), bf16),
            pltpu.VMEM((ROWS, 128), jnp.float32),
            pltpu.VMEM((ROWS, D), bf16),
        ]
        + [pltpu.VMEM(shape, bf16) for shape in outs]
        + [pltpu.SemaphoreType.DMA((7,))],
        compiler_params=pltpu.CompilerParams(vmem_limit_bytes=VMEM_LIMIT),
        cost_estimate=pl.CostEstimate(
            flops=10 * ROWS * RANK * D, bytes_accessed=16 * ROWS * D, transcendentals=ROWS * RANK
        ),
        name="local",
    )(y, recv, live, gain, stash, back_in, down, up)


def _compact(wiring, blocks, out, sems):
    for slot in range(SLOTS):

        @pl.when(slot < wiring[SLOTS])
        def _(slot=slot):
            pltpu.make_async_copy(blocks.at[wiring[slot]], out.at[slot], sems.at[slot]).start()

    for slot in range(SLOTS):
        live = slot < wiring[SLOTS]

        @pl.when(jnp.logical_not(live))
        def _(slot=slot):
            out[slot] = jnp.zeros((MB, D), jnp.bfloat16)

        @pl.when(live)
        def _(slot=slot):
            pltpu.make_async_copy(blocks.at[wiring[slot]], out.at[slot], sems.at[slot]).wait()


def compact(wiring, blocks):
    return pl.pallas_call(
        _compact,
        out_shape=jax.ShapeDtypeStruct((SLOTS, MB, D), jnp.bfloat16),
        in_specs=[pl.BlockSpec(memory_space=pltpu.SMEM), pl.BlockSpec(memory_space=pl.ANY)],
        out_specs=pl.BlockSpec(memory_space=pltpu.VMEM),
        scratch_shapes=[pltpu.SemaphoreType.DMA((SLOTS,))],
        compiler_params=pltpu.CompilerParams(vmem_limit_bytes=8 * 2**20),
        cost_estimate=pl.CostEstimate(flops=0, bytes_accessed=5 * ROWS * D, transcendentals=0),
        name="compact",
    )(wiring, blocks)


def on_device(stash, back_in, down_proj, up_proj, gain, sent_to, sent_count, recv_from, back_live):
    f32, bf16 = jnp.float32, jnp.bfloat16
    y = lax.axis_index("yl")
    swap = [(0, 1), (1, 0)]
    back = [((i + 1) % SECTIONS, i) for i in range(SECTIONS)]
    ahead = [(i, (i + 1) % SECTIONS) for i in range(SECTIONS)]
    stash = stash.reshape(ROWS, D)
    back_in = back_in.reshape(ROWS, D)
    live, recv = back_live[0, 0], recv_from[0, 0]
    by_sender, give, keep = local(
        y.astype(jnp.int32).reshape(1), recv, live, gain, stash, back_in, down_proj[0], up_proj[0]
    )
    exchanged = lax.all_to_all(by_sender, ("z", "yl"), split_axis=0, concat_axis=0, tiled=True)
    got = lax.ppermute(give, "yl", swap)
    wiring = lax.ppermute(jnp.concatenate([sent_to[0, 0], sent_count[0]]), "section", ahead)
    keep, wiring = lax.optimization_barrier((keep, wiring))
    packed = compact(wiring, exchanged)
    returned = lax.ppermute(packed, "section", back)
    pair = (keep.astype(f32) + got.astype(f32)).astype(bf16)
    pair, packed = lax.optimization_barrier((pair.reshape(180, 4096), packed))
    shard = lax.psum_scatter(pair, "z", scatter_dimension=0, tiled=True)
    mean = (shard.astype(f32) / PEERS).astype(bf16).reshape(24, HALF)
    wide, narrow = mean[:, :WIDE], mean[:, WIDE:]
    narrow_got = lax.ppermute(narrow, "yl", swap)
    narrow_both = jnp.concatenate(
        [jnp.where(y == 0, narrow, narrow_got), jnp.where(y == 0, narrow_got, narrow)], axis=1
    )
    wide, returned = lax.optimization_barrier((wide, returned))
    wide_mine = lax.all_gather(wide, "z", axis=0, tiled=True)
    wide_got = lax.ppermute(wide_mine, "yl", swap)
    narrow_both, wide_mine = lax.optimization_barrier((narrow_both, wide_mine))
    narrow_all = lax.all_gather(narrow_both, "z", axis=0, tiled=True)
    grads = jnp.concatenate(
        [
            jnp.where(y == 0, wide_mine, wide_got),
            narrow_all[:, :NARROW],
            jnp.where(y == 0, wide_got, wide_mine),
            narrow_all[:, NARROW:],
        ],
        axis=1,
    )
    return (
        returned.reshape(1, 1, SLOTS, MB, D),
        grads[None, :RANK],
        grads[None, RANK:],
    )


def solution(mesh):
    inner = Mesh(mesh.devices.reshape(SECTIONS, Z, Y), ("section", "z", "yl"))
    peer = ("z", "yl")
    placed = (
        P("section", peer, None, None, None),
        P("section", peer, None, None, None),
        P("section", None, None),
        P("section", None, None),
        P("section", None),
        P("section", peer, None),
        P("section", peer),
        P("section", peer, None),
        P("section", peer, None),
    )
    return jax.shard_map(
        on_device,
        mesh=inner,
        in_specs=placed,
        out_specs=(
            P("section", peer, None, None, None),
            P("section", None, None),
            P("section", None, None),
        ),
        check_vma=False,
    )
```

```python
import jax
import jax.numpy as jnp
from jax import lax
from jax.experimental import pallas as pl
from jax.experimental.pallas import tpu as pltpu
from jax.sharding import Mesh, PartitionSpec as P

epsilon = 1e-05
SECTIONS, Z, Y = 32, 12, 2
PEERS = Z * Y
SLOTS, MB, D, RANK = 18, 8, 5120, 144
ROWS = SLOTS * MB
HALF = D // 2
CHUNK = 512
WIDE = 1792
NARROW = HALF - WIDE
LAST = (((1,), (1,)), ((), ()))
FIRST = (((0,), (0,)), ((), ()))
VMEM_LIMIT = 60 * 2**20


def _chunks(width, step):
    return [slice(c, c + step) for c in range(0, width, step)]


def _cotangents(
    recv_ref, live_ref, gain, stash_hbm, back_in_hbm, down_hbm, up_hbm,
    out_hbm, normed_hbm, back_pre, activation,
    stash, back_in, down, up, mask, normed, out, sems,
):
    f32, bf16 = jnp.float32, jnp.bfloat16
    pairs = ((stash_hbm, stash), (down_hbm, down), (back_in_hbm, back_in), (up_hbm, up))
    loads = [pltpu.make_async_copy(a, b, sems.at[i]) for i, (a, b) in enumerate(pairs)]
    for load in loads:
        load.start()
    for slot in range(SLOTS):
        mask[MB * slot : MB * (slot + 1), :] = jnp.full((MB, 128), live_ref[slot].astype(f32), f32)
    for peer in range(PEERS):
        out[peer] = jnp.zeros((MB, D), bf16)
    loads[0].wait()
    squares = jnp.zeros((ROWS, 128), f32)
    for cols in _chunks(D, 128):
        s = stash[:, cols].astype(f32)
        squares += s * s
    live = mask[:, :1]
    inverse = lax.rsqrt(jnp.sum(squares, axis=1, keepdims=True) * (1.0 / D) + epsilon) * live
    for load in loads[1:]:
        load.wait()
    preact = jnp.zeros((ROWS, RANK), f32)
    back_act = jnp.zeros((ROWS, RANK), f32)
    for cols in _chunks(D, CHUNK):
        n = (stash[:, cols].astype(f32) * inverse * gain[:, cols]).astype(bf16)
        normed[:, cols] = n
        preact += lax.dot_general(n, down[:, cols], LAST, preferred_element_type=f32)
        back_act += lax.dot_general(back_in[:, cols], up[:, cols], LAST, preferred_element_type=f32)
    stores = [pltpu.make_async_copy(normed, normed_hbm, sems.at[4])]
    stores[0].start()
    sigmoid = 1.0 / (1.0 + jnp.exp(-preact))
    activation[...] = (preact * sigmoid).astype(bf16)
    pre = (back_act * live * (sigmoid * (1.0 + preact * (1.0 - sigmoid)))).astype(bf16)
    back_pre[...] = pre
    shared = jnp.sum(pre.astype(f32) * preact, axis=1, keepdims=True) * (inverse * (1.0 / D))
    alive = live > 0.5
    for half in range(2):
        for part in _chunks(HALF, CHUNK):
            cols = slice(half * HALF + part.start, half * HALF + part.stop)
            back_norm = jnp.dot(pre, down[:, cols], preferred_element_type=f32) * gain[:, cols]
            unit = stash[:, cols].astype(f32) * inverse
            grad = back_in[:, cols].astype(f32) + inverse * back_norm - unit * shared
            grad = jnp.where(alive, grad, 0.0)
            for slot in range(SLOTS):
                out[recv_ref[slot], :, cols] = grad[MB * slot : MB * (slot + 1), :].astype(bf16)
        here = pl.ds(half * HALF, HALF)
        stores.append(
            pltpu.make_async_copy(out.at[:, :, here], out_hbm.at[:, :, here], sems.at[5 + half])
        )
        stores[-1].start()
    for store in stores:
        store.wait()


def cotangents(recv, live, gain, stash, back_in, down, up):
    smem = pl.BlockSpec(memory_space=pltpu.SMEM)
    vmem = pl.BlockSpec(memory_space=pltpu.VMEM)
    hbm = pl.BlockSpec(memory_space=pl.ANY)
    bf16 = jnp.bfloat16
    return pl.pallas_call(
        _cotangents,
        out_shape=(
            jax.ShapeDtypeStruct((PEERS, MB, D), bf16),
            jax.ShapeDtypeStruct((ROWS, D), bf16),
            jax.ShapeDtypeStruct((ROWS, RANK), bf16),
            jax.ShapeDtypeStruct((ROWS, RANK), bf16),
        ),
        in_specs=[smem, smem, vmem] + [hbm] * 4,
        out_specs=[hbm, hbm, vmem, vmem],
        scratch_shapes=[
            pltpu.VMEM((ROWS, D), bf16),
            pltpu.VMEM((ROWS, D), bf16),
            pltpu.VMEM((RANK, D), bf16),
            pltpu.VMEM((RANK, D), bf16),
            pltpu.VMEM((ROWS, 128), jnp.float32),
            pltpu.VMEM((ROWS, D), bf16),
            pltpu.VMEM((PEERS, MB, D), bf16),
            pltpu.SemaphoreType.DMA((7,)),
        ],
        compiler_params=pltpu.CompilerParams(vmem_limit_bytes=VMEM_LIMIT),
        cost_estimate=pl.CostEstimate(
            flops=6 * ROWS * RANK * D, bytes_accessed=14 * ROWS * D, transcendentals=ROWS * RANK
        ),
        name="cotangents",
    )(recv, live, gain, stash, back_in, down, up)


def _gradients(y_ref, normed, back_in, back_pre, activation, give, keep):
    f32, bf16 = jnp.float32, jnp.bfloat16
    pre, act = back_pre[...], activation[...]
    y = y_ref[0]
    for out, half in ((give, 1 - y), (keep, y)):
        for cols in _chunks(HALF, CHUNK):
            here = pl.ds(pl.multiple_of(half * HALF + cols.start, 128), CHUNK)
            out[:RANK, cols] = lax.dot_general(
                pre, normed[:, here], FIRST, preferred_element_type=f32
            ).astype(bf16)
            out[RANK:, cols] = lax.dot_general(
                act, back_in[:, here], FIRST, preferred_element_type=f32
            ).astype(bf16)


def gradients(y, normed, back_in, back_pre, activation):
    vmem = pl.BlockSpec(memory_space=pltpu.VMEM)
    return pl.pallas_call(
        _gradients,
        out_shape=(
            jax.ShapeDtypeStruct((2 * RANK, HALF), jnp.bfloat16),
            jax.ShapeDtypeStruct((2 * RANK, HALF), jnp.bfloat16),
        ),
        in_specs=[pl.BlockSpec(memory_space=pltpu.SMEM)] + [vmem] * 4,
        out_specs=[vmem] * 2,
        compiler_params=pltpu.CompilerParams(vmem_limit_bytes=VMEM_LIMIT),
        cost_estimate=pl.CostEstimate(
            flops=4 * ROWS * RANK * D, bytes_accessed=8 * ROWS * D, transcendentals=0
        ),
        name="gradients",
    )(y, normed, back_in, back_pre, activation)


def _compact(wiring, blocks, out, sems):
    for slot in range(SLOTS):

        @pl.when(slot < wiring[SLOTS])
        def _(slot=slot):
            pltpu.make_async_copy(blocks.at[wiring[slot]], out.at[slot], sems.at[slot]).start()

    for slot in range(SLOTS):
        live = slot < wiring[SLOTS]

        @pl.when(jnp.logical_not(live))
        def _(slot=slot):
            out[slot] = jnp.zeros((MB, D), jnp.bfloat16)

        @pl.when(live)
        def _(slot=slot):
            pltpu.make_async_copy(blocks.at[wiring[slot]], out.at[slot], sems.at[slot]).wait()


def compact(wiring, blocks):
    return pl.pallas_call(
        _compact,
        out_shape=jax.ShapeDtypeStruct((SLOTS, MB, D), jnp.bfloat16),
        in_specs=[pl.BlockSpec(memory_space=pltpu.SMEM), pl.BlockSpec(memory_space=pl.ANY)],
        out_specs=pl.BlockSpec(memory_space=pltpu.VMEM),
        scratch_shapes=[pltpu.SemaphoreType.DMA((SLOTS,))],
        compiler_params=pltpu.CompilerParams(vmem_limit_bytes=8 * 2**20),
        cost_estimate=pl.CostEstimate(flops=0, bytes_accessed=5 * ROWS * D, transcendentals=0),
        name="compact",
    )(wiring, blocks)


def on_device(stash, back_in, down_proj, up_proj, gain, sent_to, sent_count, recv_from, back_live):
    f32, bf16 = jnp.float32, jnp.bfloat16
    y = lax.axis_index("yl")
    side = y.astype(jnp.int32).reshape(1)
    swap = [(0, 1), (1, 0)]
    back = [((i + 1) % SECTIONS, i) for i in range(SECTIONS)]
    ahead = [(i, (i + 1) % SECTIONS) for i in range(SECTIONS)]
    stash = stash.reshape(ROWS, D)
    back_in = back_in.reshape(ROWS, D)
    live, recv = back_live[0, 0], recv_from[0, 0]
    by_sender, normed, back_pre, activation = cotangents(
        recv, live, gain, stash, back_in, down_proj[0], up_proj[0]
    )
    exchanged = lax.all_to_all(by_sender, ("z", "yl"), split_axis=0, concat_axis=0, tiled=True)
    give, keep = gradients(side, normed, back_in, back_pre, activation)
    got = lax.ppermute(give, "yl", swap)
    wiring = lax.ppermute(jnp.concatenate([sent_to[0, 0], sent_count[0]]), "section", ahead)
    keep, wiring = lax.optimization_barrier((keep, wiring))
    packed = compact(wiring, exchanged)
    returned = lax.ppermute(packed, "section", back)
    pair = (keep.astype(f32) + got.astype(f32)).astype(bf16)
    pair, packed = lax.optimization_barrier((pair.reshape(180, 4096), packed))
    shard = lax.psum_scatter(pair, "z", scatter_dimension=0, tiled=True)
    mean = (shard.astype(f32) / PEERS).astype(bf16).reshape(24, HALF)
    wide, narrow = mean[:, :WIDE], mean[:, WIDE:]
    narrow_got = lax.ppermute(narrow, "yl", swap)
    narrow_both = jnp.concatenate(
        [jnp.where(y == 0, narrow, narrow_got), jnp.where(y == 0, narrow_got, narrow)], axis=1
    )
    wide, returned = lax.optimization_barrier((wide, returned))
    wide_mine = lax.all_gather(wide, "z", axis=0, tiled=True)
    wide_got = lax.ppermute(wide_mine, "yl", swap)
    narrow_both, wide_mine = lax.optimization_barrier((narrow_both, wide_mine))
    narrow_all = lax.all_gather(narrow_both, "z", axis=0, tiled=True)
    grads = jnp.concatenate(
        [
            jnp.where(y == 0, wide_mine, wide_got),
            narrow_all[:, :NARROW],
            jnp.where(y == 0, wide_got, wide_mine),
            narrow_all[:, NARROW:],
        ],
        axis=1,
    )
    return (
        returned.reshape(1, 1, SLOTS, MB, D),
        grads[None, :RANK],
        grads[None, RANK:],
    )


def solution(mesh):
    inner = Mesh(mesh.devices.reshape(SECTIONS, Z, Y), ("section", "z", "yl"))
    peer = ("z", "yl")
    placed = (
        P("section", peer, None, None, None),
        P("section", peer, None, None, None),
        P("section", None, None),
        P("section", None, None),
        P("section", None),
        P("section", peer, None),
        P("section", peer),
        P("section", peer, None),
        P("section", peer, None),
    )
    return jax.shard_map(
        on_device,
        mesh=inner,
        in_specs=placed,
        out_specs=(
            P("section", peer, None, None, None),
            P("section", None, None),
            P("section", None, None),
        ),
        check_vma=False,
    )
```
